32 devices in a mesh: row: 16 (over z, x, core), feat: 2 (over y).
Axes of the slice: x: 2, y: 2, z: 4, core: 2. Of those that a mesh axis runs over, the one named last changes fastest.
Arguments:
- vectors: bfloat16 [40960, 1024], P('row', 'feat')
- rotation: bfloat16 [1024, 1024], P('feat')
- codes: int32 [40960, 64], P('row', 'feat'), may hold values from 0 to 255
- live_rows: int32 [16], P('row'), may hold values from 640 to 2560
Outputs:
- centroids: float32 [256, 1024], P('row', 'feat')
- grad_t: float32 [1024, 1024], P('row', 'feat')
The draws below stay inside these ranges and needn't reach their ends.
All inputs are finite; a program needn't handle non-finite values.
Results may differ from the reference program's by a relative error of at most 0.00094.
Values may be sent and summed in bfloat16 or wider, within the bound.
A program may use at most 128 MiB of HBM per device.

```python
import jax
import jax.numpy as jnp
from jax import lax

D = 1024
M = 64
K = 256
DS = 16
ROW_DEV = 2560
BLOCKS = 16
ROWS = 40960


def shared_codes(key):
    return jax.random.randint(jax.random.fold_in(key, 7), (ROWS, M), 0, K, dtype=jnp.int32)


def draw_codes(key, part):
    return shared_codes(key)


def draw_vectors(key, part):
    codes = shared_codes(key)
    table = jax.random.normal(jax.random.fold_in(key, 11), (K, D), jnp.float32)
    spread = jnp.repeat(codes, DS, axis=1)
    offset = table[spread, jnp.arange(D)[None, :]]
    values = jax.random.normal(jax.random.fold_in(key, 13), (ROWS, D), jnp.float32) + 1.5 * offset
    return values.astype(jnp.bfloat16)


def draw_rotation(key, part):
    spread = jax.random.normal(key, (D, D), jnp.float32) * 0.5 / D ** 0.5
    return (jnp.eye(D, dtype=jnp.float32) + spread).astype(jnp.bfloat16)


def draw_live_rows(key, part):
    base = jax.random.randint(key, (BLOCKS,), ROW_DEV // 4, ROW_DEV + 1, dtype=jnp.int32)
    where = jax.random.randint(jax.random.fold_in(key, 3), (), 0, BLOCKS, dtype=jnp.int32)
    return jnp.where(jnp.arange(BLOCKS, dtype=jnp.int32) == where, ROW_DEV, base).astype(jnp.int32)


def setup_inputs(seed: int = 0) -> dict:
    key_list = jax.random.split(jax.random.key(seed), 5)
    return {
        "vectors": draw_vectors(jax.random.fold_in(key_list[4], 71), 0),
        "rotation": draw_rotation(jax.random.fold_in(key_list[4], 71), 0),
        "codes": draw_codes(jax.random.fold_in(key_list[4], 71), 0),
        "live_rows": draw_live_rows(jax.random.fold_in(key_list[4], 71), 0),
    }


def make_hot(code_block, live):
    keep = (jnp.arange(ROW_DEV, dtype=jnp.int32) < live).astype(jnp.float32)
    kinds = jnp.arange(K, dtype=jnp.int32)
    hot = (code_block[:, :, None] == kinds[None, None, :]).astype(jnp.float32) * keep[:, None, None]
    return hot.astype(jnp.bfloat16)


def reference(vectors, rotation, codes, live_rows):
    vector_blocks = vectors.reshape(BLOCKS, ROW_DEV, D)
    code_blocks = codes.reshape(BLOCKS, ROW_DEV, M)

    def first(carry, item):
        block, code_block, live = item
        rotated = jnp.dot(block, rotation, preferred_element_type=jnp.float32)
        hot = make_hot(code_block, live).astype(jnp.float32)
        pieces = rotated.reshape(ROW_DEV, M, DS)
        sums = jnp.einsum("nmk,nmd->kmd", hot, pieces, precision=lax.Precision.HIGHEST).reshape(K, D)
        counts = jnp.sum(hot, axis=0).T
        return (carry[0] + sums, carry[1] + counts), None

    start = (jnp.zeros((K, D), jnp.float32), jnp.zeros((K, M), jnp.float32))
    totals, unused = lax.scan(first, start, (vector_blocks, code_blocks, live_rows))
    sums, counts = totals
    centroids = sums / (jnp.repeat(counts, DS, axis=1) + 1.0)
    table = centroids.astype(jnp.bfloat16).astype(jnp.float32).reshape(K, M, DS)

    def second(carry, item):
        block, code_block, live = item
        hot = make_hot(code_block, live).astype(jnp.float32)
        recon = jnp.einsum("nmk,kmd->nmd", hot, table).reshape(ROW_DEV, D).astype(jnp.bfloat16)
        return carry + jnp.dot(recon.T, block, preferred_element_type=jnp.float32), None

    grad_sum, unused = lax.scan(second, jnp.zeros((D, D), jnp.float32), (vector_blocks, code_blocks, live_rows))
    return centroids, grad_sum / ROWS
```

```python
import functools

import jax
import jax.numpy as jnp
from jax import lax
from jax.experimental import pallas as pl
from jax.experimental.pallas import tpu as pltpu
from jax.sharding import PartitionSpec as P

K = 256
DS = 16
LANES = 128
PER = LANES // DS
MESH = pl.DeviceIdType.MESH
F32 = jnp.float32
BF16 = jnp.bfloat16


def one_hot(code_row, kinds):
    return jnp.where(code_row.astype(BF16) == kinds, 1.0, 0.0).astype(BF16)


def kernel(
    n_row, n_feat, inverse,
    v_ref, r_ref, codes_ref, cent_ref, grad_ref,
    code_in, codes_all, weights, kinds_ref,
    part, got_core, sum_core, got_feat, sum_feat, got_x, sum_x, got_z,
    table, table_t, recon,
    g_part, g_got_core, g_sum_core, g_got_x, g_sum_x, g_got_z,
    code_sems, s_core, s_feat, s_x, s_z, t_z, t_x, t_feat, t_core, g_core, g_x, g_z,
):
    rows, local = v_ref.shape
    groups = codes_ref.shape[0]
    deep = n_row // 4
    own = K // n_row
    tiles = local // LANES
    me_r, me_f = lax.axis_index("row"), lax.axis_index("feat")
    core, x, z = me_r % 2, (me_r // 2) % 2, me_r // 4

    def at(zz, xx, cc):
        return {"row": (zz * 2 + xx) * 2 + cc}

    sib_core, sib_x = at(z, x, 1 - core), at(z, 1 - x, core)
    z_peers = [at((z + s) % deep, x, core) for s in range(1, deep)]
    f_peers = [{"feat": (me_f + s) % n_feat} for s in range(1, n_feat)]

    barrier = pltpu.get_barrier_semaphore()
    everyone = [sib_core, sib_x] + z_peers + f_peers
    for peer in everyone:
        pl.semaphore_signal(barrier, inc=1, device_id=peer, device_id_type=MESH)
    pl.semaphore_wait(barrier, len(everyone))

    def remote(src, dst, sems, peer):
        return pltpu.make_async_remote_copy(
            src_ref=src, dst_ref=dst, send_sem=sems.at[0], recv_sem=sems.at[1],
            device_id=peer, device_id_type=MESH,
        )

    sends = [
        remote(codes_ref, code_in.at[s], code_sems.at[s], f_peers[s])
        for s in range(n_feat - 1)
    ]
    for copy in sends:
        copy.start()
    place = lax.broadcasted_iota(jnp.int32, (K, LANES), 0)
    chunk, inside = place // own, place % own
    pz, px, pc = chunk % deep, (chunk // deep) % 2, chunk // (2 * deep)
    kinds_ref[...] = (((pz * 2 + px) * 2 + pc) * own + inside).astype(F32).astype(BF16)
    codes_all[pl.ds(pl.multiple_of(me_f * groups, 8), groups), :] = codes_ref[...].astype(F32)
    for s in range(n_feat - 1):
        sends[s].wait()
        source = (me_f - (s + 1) + n_feat) % n_feat
        codes_all[pl.ds(pl.multiple_of(source * groups, 8), groups), :] = code_in[s].astype(F32)

    def hot_of(row):
        kinds = jnp.concatenate([kinds_ref[...]] * (rows // LANES), axis=1)
        return one_hot(codes_all[pl.ds(row, 1), :], kinds)

    lane = lax.broadcasted_iota(jnp.int32, (1, LANES), 1)

    def build(f, q):
        column = pl.multiple_of(f * local + q * LANES, LANES)
        rot = jnp.dot(v_ref[...], r_ref[:, pl.ds(column, LANES)], preferred_element_type=F32)
        high = rot.astype(BF16)
        low = pltpu.roll(rot - high.astype(F32), LANES // 2, 1)
        for side in range(2):
            weights[side, :, :LANES] = high
        weights[0, :, LANES:] = jnp.where(lane < LANES // 2, 1.0, low).astype(BF16)
        weights[1, :, LANES:] = jnp.where(lane < LANES // 2, low, 1.0).astype(BF16)

    def sum_tile(df, q):
        f = (me_f + df) % n_feat
        build(f, q)

        def one(i, carry):
            hot = hot_of(f * groups + q * PER + i)
            both = jnp.dot(hot, weights[i // (PER // 2)], preferred_element_type=F32)
            mine = lane // DS == i
            first, second = both[:, :LANES], both[:, LANES:]
            total = first + pltpu.roll(second, LANES // 2, 1)
            part[q, df] = jnp.where(mine, total, part[q, df])

            @pl.when(df == 0)
            def _():
                part[q, n_feat] = jnp.where(mine, second, part[q, n_feat])

            return carry

        lax.fori_loop(0, PER, one, 0)

    half, quarter = K // 2, K // 4

    def core_copy(q):
        return remote(
            part.at[q, :, pl.ds((1 - core) * half, half)], got_core.at[q], s_core.at[q], sib_core
        )

    def feat_copies(q):
        return [
            remote(sum_core.at[q, s], got_feat.at[q, s - 1], s_feat.at[q, s - 1], f_peers[s - 1])
            for s in range(1, n_feat)
        ]

    def x_copy(q):
        return remote(
            sum_feat.at[q, :, pl.ds((1 - x) * quarter, quarter)], got_x.at[q], s_x.at[q], sib_x
        )

    def z_copies(q):
        return [
            remote(
                sum_x.at[q, :, pl.ds(((z + s) % deep) * own, own)], got_z.at[q, s - 1],
                s_z.at[q, s - 1], z_peers[s - 1],
            )
            for s in range(1, deep)
        ]

    def stage(s, q):
        if s == 0:
            core_copy(q).start()
        elif s == 1:
            core_copy(q).wait()
            sum_core[q] = part[q, :, pl.ds(core * half, half)] + got_core[q]
            for copy in feat_copies(q):
                copy.start()
        elif s == 2:
            for copy in feat_copies(q):
                copy.wait()
            total = sum_core[q, 0]
            for i in range(n_feat - 1):
                total = total + got_feat[q, i]
            sum_feat[q, 0] = total
            sum_feat[q, 1] = sum_core[q, n_feat]
            x_copy(q).start()
        elif s == 3:
            x_copy(q).wait()
            sum_x[q] = sum_feat[q, :, pl.ds(x * quarter, quarter)] + got_x[q]
            for copy in z_copies(q):
                copy.start()
        else:
            for copy in z_copies(q):
                copy.wait()
            total = sum_x[q, :, pl.ds(z * own, own)]
            for i in range(deep - 1):
                total = total + got_z[q, i]
            mean = total[0] / (total[1] + 1.0)
            columns = pl.ds(pl.multiple_of(q * LANES, LANES), LANES)
            cent_ref[:, columns] = mean
            table[core, me_f, x, z, :, columns] = mean.astype(BF16)

    steps = tiles * n_feat

    def first_phase(t, carry):
        for s in range(5):
            g = t - n_feat - s

            @pl.when((g >= 0) & (g % n_feat == 0) & (g // n_feat < tiles))
            def _():
                stage(s, g // n_feat)

        @pl.when(t < steps)
        def _():
            sum_tile((n_feat - 1) - t % n_feat, t // n_feat)

        return carry

    lax.fori_loop(0, steps + 5, first_phase, 0)

    def gather(copies):
        for copy in copies:
            copy.start()
        for copy in copies:
            copy.wait()

    def same(piece, sems, peer):
        return remote(piece, piece, sems, peer)

    gather([
        same(table.at[core, me_f, x, z], t_z.at[s], z_peers[s]) for s in range(deep - 1)
    ])
    gather([same(table.at[core, me_f, x], t_x, sib_x)])
    gather([same(table.at[core, me_f], t_feat.at[s], f_peers[s]) for s in range(n_feat - 1)])
    gather([same(table.at[core], t_core, sib_core)])
    for f in range(n_feat):
        for q in range(tiles):
            block = table[:, f, :, :, :, q * LANES:(q + 1) * LANES].astype(F32).reshape(K, LANES)
            table_t[pl.ds(f * local + q * LANES, LANES), :] = block.T.astype(BF16)

    rounds = grad_ref.shape[0] // DS
    g_rows = n_row * DS
    g_half, g_quarter = g_rows // 2, g_rows // 4

    def g_core_copy(j):
        return remote(
            g_part.at[j, pl.ds((1 - core) * g_half, g_half)], g_got_core.at[j], g_core.at[j], sib_core
        )

    def g_x_copy(j):
        return remote(
            g_sum_core.at[j, pl.ds((1 - x) * g_quarter, g_quarter)], g_got_x.at[j], g_x.at[j], sib_x
        )

    def g_z_copies(j):
        return [
            remote(
                g_sum_x.at[j, pl.ds(((z + s) % deep) * DS, DS)], g_got_z.at[j, s - 1],
                g_z.at[j, s - 1], z_peers[s - 1],
            )
            for s in range(1, deep)
        ]

    def g_stage(s, j):
        if s == 0:
            g_core_copy(j).start()
        elif s == 1:
            g_core_copy(j).wait()
            g_sum_core[j] = g_part[j, pl.ds(core * g_half, g_half)] + g_got_core[j]
            g_x_copy(j).start()
        elif s == 2:
            g_x_copy(j).wait()
            g_sum_x[j] = g_sum_core[j, pl.ds(x * g_quarter, g_quarter)] + g_got_x[j]
            for copy in g_z_copies(j):
                copy.start()
        else:
            for copy in g_z_copies(j):
                copy.wait()
            total = g_sum_x[j, pl.ds(z * DS, DS)]
            for i in range(deep - 1):
                total = total + g_got_z[j, i]
            grad_ref[pl.ds(pl.multiple_of(j * DS, DS), DS), :] = total

    def rebuild(j, lo, count):
        def one(i, carry):
            p = lo + i
            pz, px, pc = p % deep, (p // deep) % 2, p // (2 * deep)
            m = ((pz * 2 + px) * 2 + pc) * rounds + j
            part_t = table_t[pl.ds(pl.multiple_of(m * DS, DS), DS), :]
            made = jnp.dot(part_t, hot_of(m), preferred_element_type=F32)
            recon[pl.ds(pl.multiple_of(p * DS, DS), DS), :] = made.astype(BF16)
            return carry

        lax.fori_loop(0, count, one, 0)

    def second_phase(t, carry):
        for s in range(4):
            g = t - 2 - s

            @pl.when((g >= 0) & (g % 2 == 0) & (g // 2 < rounds))
            def _():
                g_stage(s, g // 2)

        @pl.when(t < 2 * rounds)
        def _():
            j = t // 2
            rebuild(j, (t % 2) * (n_row // 2), n_row // 2)

            @pl.when(t % 2 == 1)
            def _():
                g_part[j] = inverse * jnp.dot(
                    recon[...], v_ref[...], preferred_element_type=F32
                )

        return carry

    lax.fori_loop(0, 2 * rounds + 4, second_phase, 0)


def shards(vectors, rotation, codes, live_rows):
    rows, local = vectors.shape
    groups = codes.shape[1]
    n_row, n_feat = lax.axis_size("row"), lax.axis_size("feat")
    deep, own, tiles = n_row // 4, K // n_row, local // LANES
    out_rows = n_feat * local // n_row
    rounds, g_rows = out_rows // DS, n_row * DS
    keep = jnp.arange(rows, dtype=jnp.int32) < live_rows[0]
    coded = jnp.where(keep[:, None], codes, -1).astype(BF16).T
    vmem = pltpu.VMEM
    sem = pltpu.SemaphoreType.DMA
    return pl.pallas_call(
        functools.partial(kernel, n_row, n_feat, 1.0 / (rows * n_row)),
        out_shape=(
            jax.ShapeDtypeStruct((own, local), F32),
            jax.ShapeDtypeStruct((out_rows, local), F32),
        ),
        in_specs=[pl.BlockSpec(memory_space=vmem)] * 3,
        out_specs=(pl.BlockSpec(memory_space=vmem),) * 2,
        scratch_shapes=[
            vmem((max(n_feat - 1, 1), groups, rows), BF16),
            vmem((n_feat * groups, rows), F32),
            vmem((2, rows, 2 * LANES), BF16),
            vmem((K, LANES), BF16),
            vmem((tiles, n_feat + 1, K, LANES), F32),
            vmem((tiles, n_feat + 1, K // 2, LANES), F32),
            vmem((tiles, n_feat + 1, K // 2, LANES), F32),
            vmem((tiles, max(n_feat - 1, 1), K // 2, LANES), F32),
            vmem((tiles, 2, K // 2, LANES), F32),
            vmem((tiles, 2, K // 4, LANES), F32),
            vmem((tiles, 2, K // 4, LANES), F32),
            vmem((tiles, max(deep - 1, 1), 2, own, LANES), F32),
            vmem((2, n_feat, 2, deep, own, local), BF16),
            vmem((n_feat * local, K), BF16),
            vmem((g_rows, rows), BF16),
            vmem((rounds, g_rows, local), F32),
            vmem((rounds, g_rows // 2, local), F32),
            vmem((rounds, g_rows // 2, local), F32),
            vmem((rounds, g_rows // 4, local), F32),
            vmem((rounds, g_rows // 4, local), F32),
            vmem((rounds, max(deep - 1, 1), DS, local), F32),
            sem((max(n_feat - 1, 1), 2)),
            sem((tiles, 2)),
            sem((tiles, max(n_feat - 1, 1), 2)),
            sem((tiles, 2)),
            sem((tiles, max(deep - 1, 1), 2)),
            sem((max(deep - 1, 1), 2)),
            sem((2,)),
            sem((max(n_feat - 1, 1), 2)),
            sem((2,)),
            sem((rounds, 2)),
            sem((rounds, 2)),
            sem((rounds, max(deep - 1, 1), 2)),
        ],
        compiler_params=pltpu.CompilerParams(
            collective_id=0, has_side_effects=True, vmem_limit_bytes=56 * 1024 * 1024
        ),
    )(vectors, rotation, coded)


def solution(mesh):
    return jax.shard_map(
        shards,
        mesh=mesh,
        in_specs=(P("row", "feat"), P("feat", None), P("row", "feat"), P("row")),
        out_specs=(P("row", "feat"), P("row", "feat")),
        check_vma=False,
    )
```

```python
import functools

import jax
import jax.numpy as jnp
from jax import lax
from jax.experimental import pallas as pl
from jax.experimental.pallas import tpu as pltpu
from jax.sharding import PartitionSpec as P

K = 256
DS = 16
LANES = 128
PER = LANES // DS
MESH = pl.DeviceIdType.MESH
F32 = jnp.float32
BF16 = jnp.bfloat16


def one_hot(code_row, kinds):
    return jnp.where(code_row.astype(BF16) == kinds, jnp.ones((), BF16), jnp.zeros((), BF16))


def kernel(
    n_row, n_feat, inverse,
    v_ref, r_ref, codes_ref, cent_ref, grad_ref,
    code_in, codes_all, weights, sums_t, counts_t, kinds_ref,
    part, got_core, sum_core, got_feat, sum_feat, got_x, sum_x, got_z,
    table, table_t, recon,
    g_part, g_got_core, g_sum_core, g_got_x, g_sum_x, g_got_z,
    code_sems, s_core, s_feat, s_x, s_z, t_z, t_x, t_feat, t_core, g_core, g_x, g_z,
):
    rows, local = v_ref.shape
    groups = codes_ref.shape[0]
    deep = n_row // 4
    own = K // n_row
    tiles = local // LANES
    me_r, me_f = lax.axis_index("row"), lax.axis_index("feat")
    core, x, z = me_r % 2, (me_r // 2) % 2, me_r // 4

    def at(zz, xx, cc):
        return {"row": (zz * 2 + xx) * 2 + cc}

    sib_core, sib_x = at(z, x, 1 - core), at(z, 1 - x, core)
    z_peers = [at((z + s) % deep, x, core) for s in range(1, deep)]
    f_peers = [{"feat": (me_f + s) % n_feat} for s in range(1, n_feat)]

    barrier = pltpu.get_barrier_semaphore()
    everyone = [sib_core, sib_x] + z_peers + f_peers
    for peer in everyone:
        pl.semaphore_signal(barrier, inc=1, device_id=peer, device_id_type=MESH)
    pl.semaphore_wait(barrier, len(everyone))

    def remote(src, dst, sems, peer):
        return pltpu.make_async_remote_copy(
            src_ref=src, dst_ref=dst, send_sem=sems.at[0], recv_sem=sems.at[1],
            device_id=peer, device_id_type=MESH,
        )

    sends = [
        remote(codes_ref, code_in.at[s], code_sems.at[s], f_peers[s])
        for s in range(n_feat - 1)
    ]
    for copy in sends:
        copy.start()
    place = lax.broadcasted_iota(jnp.int32, (K, LANES), 0)
    chunk, inside = place // own, place % own
    pz, px, pc = chunk % deep, (chunk // deep) % 2, chunk // (2 * deep)
    kinds_ref[...] = (((pz * 2 + px) * 2 + pc) * own + inside).astype(F32).astype(BF16)
    codes_all[pl.ds(pl.multiple_of(me_f * groups, 8), groups), :] = codes_ref[...].astype(F32)
    for s in range(n_feat - 1):
        sends[s].wait()
        source = (me_f - (s + 1) + n_feat) % n_feat
        codes_all[pl.ds(pl.multiple_of(source * groups, 8), groups), :] = code_in[s].astype(F32)

    def hot_of(row):
        kinds = jnp.concatenate([kinds_ref[...]] * (rows // LANES), axis=1)
        return one_hot(codes_all[pl.ds(row, 1), :], kinds)

    nt = (((1,), (1,)), ((), ()))
    weights[:, 2 * DS:, :] = jnp.ones((PER, DS, rows), BF16)

    def build(f, q):
        column = pl.multiple_of(f * local + q * LANES, LANES)
        turned = r_ref[:, pl.ds(column, LANES)].astype(F32).T.astype(BF16)
        rot = lax.dot_general(turned, v_ref[...], nt, preferred_element_type=F32)
        high = rot.astype(BF16)
        low = (rot - high.astype(F32)).astype(BF16)
        for i in range(PER):
            weights[i, :DS] = high[i * DS:(i + 1) * DS]
            weights[i, DS:2 * DS] = low[i * DS:(i + 1) * DS]

    def sum_tile(df, q):
        f = (me_f + df) % n_feat
        build(f, q)

        def one(i, carry):
            hot = hot_of(f * groups + q * PER + i)
            both = lax.dot_general(weights[i], hot, nt, preferred_element_type=F32)
            features = pl.ds(pl.multiple_of(i * DS, DS), DS)
            sums_t[features, :] = both[:DS] + both[DS:2 * DS]
            counts_t[features, :] = both[2 * DS:]
            return carry

        lax.fori_loop(0, PER, one, 0)
        part[q, df] = sums_t[...].T

        @pl.when(df == 0)
        def _():
            part[q, n_feat] = counts_t[...].T

    half, quarter = K // 2, K // 4

    def core_copy(q):
        return remote(
            part.at[q, :, pl.ds((1 - core) * half, half)], got_core.at[q], s_core.at[q], sib_core
        )

    def feat_copies(q):
        return [
            remote(sum_core.at[q, s], got_feat.at[q, s - 1], s_feat.at[q, s - 1], f_peers[s - 1])
            for s in range(1, n_feat)
        ]

    def x_copy(q):
        return remote(
            sum_feat.at[q, :, pl.ds((1 - x) * quarter, quarter)], got_x.at[q], s_x.at[q], sib_x
        )

    def z_copies(q):
        return [
            remote(
                sum_x.at[q, :, pl.ds(((z + s) % deep) * own, own)], got_z.at[q, s - 1],
                s_z.at[q, s - 1], z_peers[s - 1],
            )
            for s in range(1, deep)
        ]

    def stage(s, q):
        if s == 0:
            core_copy(q).start()
        elif s == 1:
            core_copy(q).wait()
            sum_core[q] = part[q, :, pl.ds(core * half, half)] + got_core[q]
            for copy in feat_copies(q):
                copy.start()
        elif s == 2:
            for copy in feat_copies(q):
                copy.wait()
            total = sum_core[q, 0]
            for i in range(n_feat - 1):
                total = total + got_feat[q, i]
            sum_feat[q, 0] = total
            sum_feat[q, 1] = sum_core[q, n_feat]
            x_copy(q).start()
        elif s == 3:
            x_copy(q).wait()
            sum_x[q] = sum_feat[q, :, pl.ds(x * quarter, quarter)] + got_x[q]
            for copy in z_copies(q):
                copy.start()
        else:
            for copy in z_copies(q):
                copy.wait()
            total = sum_x[q, :, pl.ds(z * own, own)]
            for i in range(deep - 1):
                total = total + got_z[q, i]
            mean = total[0] / (total[1] + 1.0)
            columns = pl.ds(pl.multiple_of(q * LANES, LANES), LANES)
            cent_ref[:, columns] = mean
            table[core, me_f, x, z, :, columns] = mean.astype(BF16)

    steps = tiles * n_feat

    def first_phase(t, carry):
        for s in range(5):
            g = t - n_feat - s

            @pl.when((g >= 0) & (g % n_feat == 0) & (g // n_feat < tiles))
            def _():
                stage(s, g // n_feat)

        @pl.when(t < steps)
        def _():
            sum_tile((n_feat - 1) - t % n_feat, t // n_feat)

        return carry

    lax.fori_loop(0, steps + 5, first_phase, 0)

    def gather(copies):
        for copy in copies:
            copy.start()
        for copy in copies:
            copy.wait()

    def same(piece, sems, peer):
        return remote(piece, piece, sems, peer)

    gather([
        same(table.at[core, me_f, x, z], t_z.at[s], z_peers[s]) for s in range(deep - 1)
    ])
    gather([same(table.at[core, me_f, x], t_x, sib_x)])
    gather([same(table.at[core, me_f], t_feat.at[s], f_peers[s]) for s in range(n_feat - 1)])
    gather([same(table.at[core], t_core, sib_core)])
    for f in range(n_feat):
        for q in range(tiles):
            block = table[:, f, :, :, :, q * LANES:(q + 1) * LANES].astype(F32).reshape(K, LANES)
            table_t[pl.ds(f * local + q * LANES, LANES), :] = block.T.astype(BF16)

    rounds = grad_ref.shape[0] // DS
    g_rows = n_row * DS
    g_half, g_quarter = g_rows // 2, g_rows // 4

    def g_core_copy(j):
        return remote(
            g_part.at[j, pl.ds((1 - core) * g_half, g_half)], g_got_core.at[j], g_core.at[j], sib_core
        )

    def g_x_copy(j):
        return remote(
            g_sum_core.at[j, pl.ds((1 - x) * g_quarter, g_quarter)], g_got_x.at[j], g_x.at[j], sib_x
        )

    def g_z_copies(j):
        return [
            remote(
                g_sum_x.at[j, pl.ds(((z + s) % deep) * DS, DS)], g_got_z.at[j, s - 1],
                g_z.at[j, s - 1], z_peers[s - 1],
            )
            for s in range(1, deep)
        ]

    def g_stage(s, j):
        if s == 0:
            g_core_copy(j).start()
        elif s == 1:
            g_core_copy(j).wait()
            g_sum_core[j] = g_part[j, pl.ds(core * g_half, g_half)] + g_got_core[j]
            g_x_copy(j).start()
        elif s == 2:
            g_x_copy(j).wait()
            g_sum_x[j] = g_sum_core[j, pl.ds(x * g_quarter, g_quarter)] + g_got_x[j]
            for copy in g_z_copies(j):
                copy.start()
        else:
            for copy in g_z_copies(j):
                copy.wait()
            total = g_sum_x[j, pl.ds(z * DS, DS)]
            for i in range(deep - 1):
                total = total + g_got_z[j, i]
            grad_ref[pl.ds(pl.multiple_of(j * DS, DS), DS), :] = total

    def rebuild(j, lo, count):
        def one(i, carry):
            p = lo + i
            pz, px, pc = p % deep, (p // deep) % 2, p // (2 * deep)
            m = ((pz * 2 + px) * 2 + pc) * rounds + j
            part_t = table_t[pl.ds(pl.multiple_of(m * DS, DS), DS), :]
            made = jnp.dot(part_t, hot_of(m), preferred_element_type=F32)
            recon[pl.ds(pl.multiple_of(p * DS, DS), DS), :] = made.astype(BF16)
            return carry

        lax.fori_loop(0, count, one, 0)

    def second_phase(t, carry):
        for s in range(4):
            g = t - 2 - s

            @pl.when((g >= 0) & (g % 2 == 0) & (g // 2 < rounds))
            def _():
                g_stage(s, g // 2)

        @pl.when(t < 2 * rounds)
        def _():
            j = t // 2
            rebuild(j, (t % 2) * (n_row // 2), n_row // 2)

            @pl.when(t % 2 == 1)
            def _():
                g_part[j] = inverse * jnp.dot(
                    recon[...], v_ref[...], preferred_element_type=F32
                )

        return carry

    lax.fori_loop(0, 2 * rounds + 4, second_phase, 0)


def shards(vectors, rotation, codes, live_rows):
    rows, local = vectors.shape
    groups = codes.shape[1]
    n_row, n_feat = lax.axis_size("row"), lax.axis_size("feat")
    deep, own, tiles = n_row // 4, K // n_row, local // LANES
    out_rows = n_feat * local // n_row
    rounds, g_rows = out_rows // DS, n_row * DS
    keep = jnp.arange(rows, dtype=jnp.int32) < live_rows[0]
    coded = jnp.where(keep[:, None], codes, -1).astype(BF16).T
    vmem = pltpu.VMEM
    sem = pltpu.SemaphoreType.DMA
    return pl.pallas_call(
        functools.partial(kernel, n_row, n_feat, 1.0 / (rows * n_row)),
        out_shape=(
            jax.ShapeDtypeStruct((own, local), F32),
            jax.ShapeDtypeStruct((out_rows, local), F32),
        ),
        in_specs=[pl.BlockSpec(memory_space=vmem)] * 3,
        out_specs=(pl.BlockSpec(memory_space=vmem),) * 2,
        scratch_shapes=[
            vmem((max(n_feat - 1, 1), groups, rows), BF16),
            vmem((n_feat * groups, rows), F32),
            vmem((PER, 3 * DS, rows), BF16),
            vmem((LANES, K), F32),
            vmem((LANES, K), F32),
            vmem((K, LANES), BF16),
            vmem((tiles, n_feat + 1, K, LANES), F32),
            vmem((tiles, n_feat + 1, K // 2, LANES), F32),
            vmem((tiles, n_feat + 1, K // 2, LANES), F32),
            vmem((tiles, max(n_feat - 1, 1), K // 2, LANES), F32),
            vmem((tiles, 2, K // 2, LANES), F32),
            vmem((tiles, 2, K // 4, LANES), F32),
            vmem((tiles, 2, K // 4, LANES), F32),
            vmem((tiles, max(deep - 1, 1), 2, own, LANES), F32),
            vmem((2, n_feat, 2, deep, own, local), BF16),
            vmem((n_feat * local, K), BF16),
            vmem((g_rows, rows), BF16),
            vmem((rounds, g_rows, local), F32),
            vmem((rounds, g_rows // 2, local), F32),
            vmem((rounds, g_rows // 2, local), F32),
            vmem((rounds, g_rows // 4, local), F32),
            vmem((rounds, g_rows // 4, local), F32),
            vmem((rounds, max(deep - 1, 1), DS, local), F32),
            sem((max(n_feat - 1, 1), 2)),
            sem((tiles, 2)),
            sem((tiles, max(n_feat - 1, 1), 2)),
            sem((tiles, 2)),
            sem((tiles, max(deep - 1, 1), 2)),
            sem((max(deep - 1, 1), 2)),
            sem((2,)),
            sem((max(n_feat - 1, 1), 2)),
            sem((2,)),
            sem((rounds, 2)),
            sem((rounds, 2)),
            sem((rounds, max(deep - 1, 1), 2)),
        ],
        compiler_params=pltpu.CompilerParams(
            collective_id=0, has_side_effects=True, vmem_limit_bytes=56 * 1024 * 1024
        ),
    )(vectors, rotation, coded)


def solution(mesh):
    return jax.shard_map(
        shards,
        mesh=mesh,
        in_specs=(P("row", "feat"), P("feat", None), P("row", "feat"), P("row")),
        out_specs=(P("row", "feat"), P("row", "feat")),
        check_vma=False,
    )
```

```python
import functools

import jax
import jax.numpy as jnp
from jax import lax
from jax.experimental import pallas as pl
from jax.experimental.pallas import tpu as pltpu
from jax.sharding import PartitionSpec as P

K = 256
DS = 16
LANES = 128
PER = LANES // DS
MESH = pl.DeviceIdType.MESH
F32 = jnp.float32
BF16 = jnp.bfloat16


def one_hot(code_row, kinds):
    return jnp.where(code_row.astype(BF16) == kinds, jnp.ones((), BF16), jnp.zeros((), BF16))


def kernel(
    n_row, n_feat, inverse,
    v_ref, r_ref, codes_ref, cent_ref, grad_ref,
    code_in, codes_all, kinds_ref, r_tiles, hots, gathered,
    part, got_core, sum_core, got_feat, sum_feat, got_x, sum_x, got_z,
    table, table_t,
    g_part, g_got_core, g_sum_core, g_got_x, g_sum_x, g_got_z,
    code_sems, s_core, s_feat, s_x, s_z, t_z, t_x, t_feat, t_core, g_core, g_x, g_z,
):
    rows, local = v_ref.shape
    groups = codes_ref.shape[0]
    deep = n_row // 4
    own = K // n_row
    tiles = local // LANES
    per = PER * n_feat // n_row
    owned = tiles * per
    batch = PER // 2
    me_r, me_f = lax.axis_index("row"), lax.axis_index("feat")
    core, x, z = me_r % 2, (me_r // 2) % 2, me_r // 4

    def at(zz, xx, cc):
        return {"row": (zz * 2 + xx) * 2 + cc}

    sib_core, sib_x = at(z, x, 1 - core), at(z, 1 - x, core)
    z_peers = [at((z + s) % deep, x, core) for s in range(1, deep)]
    f_peers = [{"feat": (me_f + s) % n_feat} for s in range(1, n_feat)]

    barrier = pltpu.get_barrier_semaphore()
    everyone = [sib_core, sib_x] + z_peers + f_peers
    for peer in everyone:
        pl.semaphore_signal(barrier, inc=1, device_id=peer, device_id_type=MESH)
    pl.semaphore_wait(barrier, len(everyone))

    def remote(src, dst, sems, peer):
        return pltpu.make_async_remote_copy(
            src_ref=src, dst_ref=dst, send_sem=sems.at[0], recv_sem=sems.at[1],
            device_id=peer, device_id_type=MESH,
        )

    sends = [
        remote(codes_ref, code_in.at[s], code_sems.at[s], f_peers[s])
        for s in range(n_feat - 1)
    ]
    for copy in sends:
        copy.start()
    place = lax.broadcasted_iota(jnp.int32, (K, LANES), 0)
    chunk, inside = place // own, place % own
    pz, px, pc = chunk % deep, (chunk // deep) % 2, chunk // (2 * deep)
    kinds_ref[...] = (((pz * 2 + px) * 2 + pc) * own + inside).astype(F32).astype(BF16)
    codes_all[pl.ds(pl.multiple_of(me_f * groups, 8), groups), :] = codes_ref[...].astype(F32)

    def member(i, q):
        return (i // per) * owned + q * per + i % per

    for f in range(n_feat):
        block = r_ref[:, f * local:(f + 1) * local].astype(F32)
        for q in range(tiles):
            r_tiles[f * tiles + q] = jnp.concatenate(
                [block[:, member(i, q) * DS:(member(i, q) + 1) * DS] for i in range(PER)], axis=1
            ).astype(BF16)
    for s in range(n_feat - 1):
        sends[s].wait()
        source = (me_f - (s + 1) + n_feat) % n_feat
        codes_all[pl.ds(pl.multiple_of(source * groups, 8), groups), :] = code_in[s].astype(F32)

    lane = lax.broadcasted_iota(jnp.int32, (1, LANES), 1)

    def sum_half(df, q, h):
        f = (me_f + df) % n_feat
        kinds = jnp.concatenate([kinds_ref[...]] * (rows // LANES), axis=1)
        ids = [f * groups + member(h * batch + i, q) for i in range(batch)]
        for i in range(batch):
            hots[i * K:(i + 1) * K, :] = one_hot(codes_all[pl.ds(ids[i], 1), :], kinds)
        full = jnp.dot(hots[...], v_ref[...], preferred_element_type=F32)
        high = full.astype(BF16)
        low = (full - high.astype(F32)).astype(BF16)
        r_tile = r_tiles[f * tiles + q]
        sums = jnp.dot(high, r_tile, preferred_element_type=F32) + jnp.dot(
            low, r_tile, preferred_element_type=F32
        )
        for i in range(batch):
            gathered[ids[i], :K] = high[i * K:(i + 1) * K]
            gathered[ids[i], K:] = low[i * K:(i + 1) * K]
            mine = lane // DS == h * batch + i
            part[q, df] = jnp.where(mine, sums[i * K:(i + 1) * K], part[q, df])

        @pl.when(df == 0)
        def _():
            ones = jnp.ones((LANES, LANES), BF16)
            for i in range(batch):
                some = hots[i * K:(i + 1) * K, :LANES]
                for c in range(1, rows // LANES):
                    some = some + hots[i * K:(i + 1) * K, c * LANES:(c + 1) * LANES]
                count = jnp.dot(some, ones, preferred_element_type=F32)
                mine = lane // DS == h * batch + i
                part[q, n_feat] = jnp.where(mine, count, part[q, n_feat])

    half, quarter = K // 2, K // 4

    def core_copy(q):
        return remote(
            part.at[q, :, pl.ds((1 - core) * half, half)], got_core.at[q], s_core.at[q], sib_core
        )

    def feat_copies(q):
        return [
            remote(sum_core.at[q, s], got_feat.at[q, s - 1], s_feat.at[q, s - 1], f_peers[s - 1])
            for s in range(1, n_feat)
        ]

    def x_copy(q):
        return remote(
            sum_feat.at[q, :, pl.ds((1 - x) * quarter, quarter)], got_x.at[q], s_x.at[q], sib_x
        )

    def z_copies(q):
        return [
            remote(
                sum_x.at[q, :, pl.ds(((z + s) % deep) * own, own)], got_z.at[q, s - 1],
                s_z.at[q, s - 1], z_peers[s - 1],
            )
            for s in range(1, deep)
        ]

    def same(piece, sems, peer):
        return remote(piece, piece, sems, peer)

    def table_z(q):
        piece = table.at[q, core, me_f, x, z]
        return [same(piece, t_z.at[q, s], z_peers[s]) for s in range(deep - 1)]

    def table_x(q):
        return [same(table.at[q, core, me_f, x], t_x.at[q], sib_x)]

    def table_feat(q):
        piece = table.at[q, core, me_f]
        return [same(piece, t_feat.at[q, s], f_peers[s]) for s in range(n_feat - 1)]

    def table_core(q):
        return [same(table.at[q, core], t_core.at[q], sib_core)]

    deal = per * DS
    g_half, g_quarter = n_row * deal // 2, n_row * deal // 4

    def g_core_copy(q):
        return remote(
            g_part.at[q, pl.ds((1 - core) * g_half, g_half)], g_got_core.at[q], g_core.at[q], sib_core
        )

    def g_x_copy(q):
        return remote(
            g_sum_core.at[q, pl.ds((1 - x) * g_quarter, g_quarter)], g_got_x.at[q], g_x.at[q], sib_x
        )

    def g_z_copies(q):
        return [
            remote(
                g_sum_x.at[q, pl.ds(((z + s) % deep) * deal, deal)], g_got_z.at[q, s - 1],
                g_z.at[q, s - 1], z_peers[s - 1],
            )
            for s in range(1, deep)
        ]

    def gradient(q):
        def one(i, carry):
            p, e = i // per, i % per
            gz, gx, gc = p % deep, (p // deep) % 2, p // (2 * deep)
            r = (gz * 2 + gx) * 2 + gc
            line = table_t[q, pl.ds(pl.multiple_of((r * per + e) * DS, DS), DS), :]
            made = jnp.dot(line, gathered[r * owned + q * per + e], preferred_element_type=F32)
            g_part[q, pl.ds(pl.multiple_of(i * DS, DS), DS), :] = made * inverse
            return carry

        lax.fori_loop(0, n_row * per, one, 0)

    def start(copies):
        for copy in copies:
            copy.start()

    def wait(copies):
        for copy in copies:
            copy.wait()

    def stage(s, q):
        if s == 0:
            core_copy(q).start()
        elif s == 1:
            core_copy(q).wait()
            sum_core[q] = part[q, :, pl.ds(core * half, half)] + got_core[q]
            start(feat_copies(q))
        elif s == 2:
            wait(feat_copies(q))
            total = sum_core[q, 0]
            for i in range(n_feat - 1):
                total = total + got_feat[q, i]
            sum_feat[q, 0] = total
            sum_feat[q, 1] = sum_core[q, n_feat]
            x_copy(q).start()
        elif s == 3:
            x_copy(q).wait()
            sum_x[q] = sum_feat[q, :, pl.ds(x * quarter, quarter)] + got_x[q]
            start(z_copies(q))
        elif s == 4:
            wait(z_copies(q))
            total = sum_x[q, :, pl.ds(z * own, own)]
            for i in range(deep - 1):
                total = total + got_z[q, i]
            mean = total[0] / (total[1] + 1.0)
            cent_ref[q] = mean
            table[q, core, me_f, x, z] = mean.astype(BF16)
            start(table_z(q))
        elif s == 5:
            wait(table_z(q))
            start(table_x(q))
        elif s == 6:
            wait(table_x(q))
            start(table_feat(q))
        elif s == 7:
            wait(table_feat(q))
            start(table_core(q))
        elif s == 8:
            wait(table_core(q))
            for f in range(n_feat):
                turned = table[q, :, f].astype(F32).reshape(K, LANES).T.astype(BF16)
                for side in range(2):
                    table_t[q, f * LANES:(f + 1) * LANES, side * K:(side + 1) * K] = turned
            gradient(q)
            g_core_copy(q).start()
        elif s == 9:
            g_core_copy(q).wait()
            g_sum_core[q] = g_part[q, pl.ds(core * g_half, g_half)] + g_got_core[q]
            g_x_copy(q).start()
        elif s == 10:
            g_x_copy(q).wait()
            g_sum_x[q] = g_sum_core[q, pl.ds(x * g_quarter, g_quarter)] + g_got_x[q]
            start(g_z_copies(q))
        else:
            wait(g_z_copies(q))
            total = g_sum_x[q, pl.ds(z * deal, deal)]
            for i in range(deep - 1):
                total = total + g_got_z[q, i]
            grad_ref[pl.ds(pl.multiple_of(q * deal, deal), deal), :] = total

    stages = 12
    each = 2 * n_feat
    steps = tiles * each

    def step(t, carry):
        for s in reversed(range(stages)):
            g = t - each - s

            @pl.when((g >= 0) & (g % each == 0) & (g // each < tiles))
            def _():
                stage(s, g // each)

        @pl.when(t < steps)
        def _():
            sum_half((n_feat - 1) - (t % each) // 2, t // each, t % 2)

        return carry

    lax.fori_loop(0, steps + stages, step, 0)


def shards(vectors, rotation, codes, live_rows):
    rows, local = vectors.shape
    groups = codes.shape[1]
    n_row, n_feat = lax.axis_size("row"), lax.axis_size("feat")
    deep, own, tiles = n_row // 4, K // n_row, local // LANES
    out_rows = n_feat * local // n_row
    per = PER * n_feat // n_row
    deal = per * DS
    g_rows = n_row * deal
    others, far = max(n_feat - 1, 1), max(deep - 1, 1)
    keep = jnp.arange(rows, dtype=jnp.int32) < live_rows[0]
    coded = jnp.where(keep[:, None], codes, -1).astype(BF16).T
    vmem = pltpu.VMEM
    sem = pltpu.SemaphoreType.DMA
    means, grad_t = pl.pallas_call(
        functools.partial(kernel, n_row, n_feat, 1.0 / (rows * n_row)),
        out_shape=(
            jax.ShapeDtypeStruct((tiles, own, LANES), F32),
            jax.ShapeDtypeStruct((out_rows, local), F32),
        ),
        in_specs=[pl.BlockSpec(memory_space=vmem)] * 3,
        out_specs=(pl.BlockSpec(memory_space=vmem),) * 2,
        scratch_shapes=[
            vmem((others, groups, rows), BF16),
            vmem((n_feat * groups, rows), F32),
            vmem((K, LANES), BF16),
            vmem((n_feat * tiles, local, LANES), BF16),
            vmem((PER // 2 * K, rows), BF16),
            vmem((n_feat * groups, 2 * K, local), BF16),
            vmem((tiles, n_feat + 1, K, LANES), F32),
            vmem((tiles, n_feat + 1, K // 2, LANES), F32),
            vmem((tiles, n_feat + 1, K // 2, LANES), F32),
            vmem((tiles, others, K // 2, LANES), F32),
            vmem((tiles, 2, K // 2, LANES), F32),
            vmem((tiles, 2, K // 4, LANES), F32),
            vmem((tiles, 2, K // 4, LANES), F32),
            vmem((tiles, far, 2, own, LANES), F32),
            vmem((tiles, 2, n_feat, 2, deep, own, LANES), BF16),
            vmem((tiles, n_feat * LANES, 2 * K), BF16),
            vmem((tiles, g_rows, local), F32),
            vmem((tiles, g_rows // 2, local), F32),
            vmem((tiles, g_rows // 2, local), F32),
            vmem((tiles, g_rows // 4, local), F32),
            vmem((tiles, g_rows // 4, local), F32),
            vmem((tiles, far, deal, local), F32),
            sem((others, 2)),
            sem((tiles, 2)),
            sem((tiles, others, 2)),
            sem((tiles, 2)),
            sem((tiles, far, 2)),
            sem((tiles, far, 2)),
            sem((tiles, 2)),
            sem((tiles, others, 2)),
            sem((tiles, 2)),
            sem((tiles, 2)),
            sem((tiles, 2)),
            sem((tiles, far, 2)),
        ],
        compiler_params=pltpu.CompilerParams(
            collective_id=0, has_side_effects=True, vmem_limit_bytes=63 * 1024 * 1024
        ),
    )(vectors, rotation, coded)
    split = means.reshape(tiles, own, PER // per, per, DS)
    return split.transpose(1, 2, 0, 3, 4).reshape(own, local), grad_t


def solution(mesh):
    return jax.shard_map(
        shards,
        mesh=mesh,
        in_specs=(P("row", "feat"), P("feat", None), P("row", "feat"), P("row")),
        out_specs=(P("row", "feat"), P("row", "feat")),
        check_vma=False,
    )
```

```python
import functools

import jax
import jax.numpy as jnp
from jax import lax
from jax.experimental import pallas as pl
from jax.experimental.pallas import tpu as pltpu
from jax.sharding import PartitionSpec as P

K = 256
DS = 16
LANES = 128
PER = LANES // DS
MESH = pl.DeviceIdType.MESH
F32 = jnp.float32
BF16 = jnp.bfloat16


def one_hot(code_row, kinds):
    return jnp.where(code_row.astype(BF16) == kinds, jnp.ones((), BF16), jnp.zeros((), BF16))


def kernel(
    n_row, n_feat, inverse,
    v_ref, r_ref, codes_ref, cent_ref, grad_ref,
    code_in, codes_all, kinds_ref, r_tiles, weights, sums_t, counts_t,
    part, got_core, sum_core, got_feat, sum_feat, got_x, sum_x, got_z,
    table, table_t, recon,
    g_part, g_got_core, g_sum_core, g_got_x, g_sum_x, g_got_z,
    code_sems, s_core, s_feat, s_x, s_z, t_z, t_x, t_feat, t_core, g_core, g_x, g_z,
):
    rows, local = v_ref.shape
    groups = codes_ref.shape[0]
    deep = n_row // 4
    own = K // n_row
    tiles = local // LANES
    per = PER * n_feat // n_row
    owned = tiles * per
    half, quarter = K // 2, K // 4
    me_r, me_f = lax.axis_index("row"), lax.axis_index("feat")
    core, x, z = me_r % 2, (me_r // 2) % 2, me_r // 4

    def at(zz, xx, cc):
        return {"row": (zz * 2 + xx) * 2 + cc}

    sib_core, sib_x = at(z, x, 1 - core), at(z, 1 - x, core)
    z_peers = [at((z + s) % deep, x, core) for s in range(1, deep)]
    f_peers = [{"feat": (me_f + s) % n_feat} for s in range(1, n_feat)]

    barrier = pltpu.get_barrier_semaphore()
    everyone = [sib_core, sib_x] + z_peers + f_peers
    for peer in everyone:
        pl.semaphore_signal(barrier, inc=1, device_id=peer, device_id_type=MESH)
    pl.semaphore_wait(barrier, len(everyone))

    def remote(src, dst, sems, peer):
        return pltpu.make_async_remote_copy(
            src_ref=src, dst_ref=dst, send_sem=sems.at[0], recv_sem=sems.at[1],
            device_id=peer, device_id_type=MESH,
        )

    sends = [
        remote(codes_ref, code_in.at[s], code_sems.at[s], f_peers[s])
        for s in range(n_feat - 1)
    ]
    for copy in sends:
        copy.start()
    kinds_ref[...] = lax.broadcasted_iota(jnp.int32, (half, LANES), 0).astype(F32).astype(BF16)
    weights[:, 2 * DS:, :] = jnp.ones((n_feat * PER, DS, rows), BF16)
    codes_all[pl.ds(pl.multiple_of(me_f * groups, 8), groups), :] = codes_ref[...].astype(F32)

    def member(i, q):
        return (i // per) * owned + q * per + i % per

    for f in range(n_feat):
        block = r_ref[:, f * local:(f + 1) * local].astype(F32)
        for q in range(tiles):
            r_tiles[q, f * LANES:(f + 1) * LANES] = jnp.concatenate(
                [block[:, member(i, q) * DS:(member(i, q) + 1) * DS] for i in range(PER)], axis=1
            ).T.astype(BF16)
    for s in range(n_feat - 1):
        sends[s].wait()
        source = (me_f - (s + 1) + n_feat) % n_feat
        codes_all[pl.ds(pl.multiple_of(source * groups, 8), groups), :] = code_in[s].astype(F32)

    nt = (((1,), (1,)), ((), ()))

    def pair(first, second):
        kinds = jnp.concatenate([kinds_ref[...]] * (rows // LANES), axis=1)
        hots, uppers = [], []
        for m in (first, second):
            row = codes_all[pl.ds(m, 1), :]
            upper = row >= half
            hots.append(one_hot(jnp.where(upper, row - half, row), kinds))
            uppers.append(upper)
        return jnp.concatenate(hots, axis=0), uppers

    def build(q):
        rot = lax.dot_general(r_tiles[q], v_ref[...], nt, preferred_element_type=F32)
        high = rot.astype(BF16)
        low = (rot - high.astype(F32)).astype(BF16)
        for i in range(n_feat * PER):
            weights[i, :DS] = high[i * DS:(i + 1) * DS]
            weights[i, DS:2 * DS] = low[i * DS:(i + 1) * DS]

    def sum_pair(f, q, i):
        ids = [f * groups + member(i + n, q) for n in range(2)]
        hots, uppers = pair(*ids)
        lines = []
        for n in range(2):
            line = weights[f * PER + i + n]
            up = jnp.where(uppers[n], 1.0, 0.0)
            lines += [line * (1.0 - up).astype(BF16), line * up.astype(BF16)]
        made = lax.dot_general(
            jnp.concatenate(lines, axis=0), hots, nt, preferred_element_type=F32
        )
        for n in range(2):
            features = pl.ds(pl.multiple_of((i + n) * DS, DS), DS)
            for side in range(2):
                at_row = (2 * n + side) * 3 * DS
                both = made[at_row:at_row + 3 * DS, n * half:(n + 1) * half]
                positions = slice(side * half, (side + 1) * half)
                sums_t[features, positions] = both[:DS] + both[DS:2 * DS]
                counts_t[features, positions] = both[2 * DS:]

    def sum_half(df, q, h):
        f = (me_f + df) % n_feat

        def one(i, carry):
            sum_pair(f, q, h * (PER // 2) + 2 * i)
            return carry

        lax.fori_loop(0, PER // 4, one, 0)

        @pl.when(h == 1)
        def _():
            part[q, df] = sums_t[...].T

            @pl.when(df == 0)
            def _():
                part[q, n_feat] = counts_t[...].T

    def core_copy(q):
        return remote(
            part.at[q, :, pl.ds((1 - core) * half, half)], got_core.at[q], s_core.at[q], sib_core
        )

    def feat_copies(q):
        return [
            remote(sum_core.at[q, s], got_feat.at[q, s - 1], s_feat.at[q, s - 1], f_peers[s - 1])
            for s in range(1, n_feat)
        ]

    def x_copy(q):
        return remote(
            sum_feat.at[q, :, pl.ds((1 - x) * quarter, quarter)], got_x.at[q], s_x.at[q], sib_x
        )

    def z_copies(q):
        return [
            remote(
                sum_x.at[q, :, pl.ds(((z + s) % deep) * own, own)], got_z.at[q, s - 1],
                s_z.at[q, s - 1], z_peers[s - 1],
            )
            for s in range(1, deep)
        ]

    def same(piece, sems, peer):
        return remote(piece, piece, sems, peer)

    def table_z(q):
        piece = table.at[q, core, me_f, x, z]
        return [same(piece, t_z.at[q, s], z_peers[s]) for s in range(deep - 1)]

    def table_x(q):
        return [same(table.at[q, core, me_f, x], t_x.at[q], sib_x)]

    def table_feat(q):
        piece = table.at[q, core, me_f]
        return [same(piece, t_feat.at[q, s], f_peers[s]) for s in range(n_feat - 1)]

    def table_core(q):
        return [same(table.at[q, core], t_core.at[q], sib_core)]

    deal = per * DS
    g_half, g_quarter = n_row * deal // 2, n_row * deal // 4

    def g_core_copy(q):
        return remote(
            g_part.at[q, pl.ds((1 - core) * g_half, g_half)], g_got_core.at[q], g_core.at[q], sib_core
        )

    def g_x_copy(q):
        return remote(
            g_sum_core.at[q, pl.ds((1 - x) * g_quarter, g_quarter)], g_got_x.at[q], g_x.at[q], sib_x
        )

    def g_z_copies(q):
        return [
            remote(
                g_sum_x.at[q, pl.ds(((z + s) % deep) * deal, deal)], g_got_z.at[q, s - 1],
                g_z.at[q, s - 1], z_peers[s - 1],
            )
            for s in range(1, deep)
        ]

    def rebuild(q, lo):
        def one(i, carry):
            places, ids, lines = [], [], []
            blank = jnp.zeros((2 * DS, half), BF16)
            for n in range(2):
                g = lo + 2 * i + n
                p, e = g // per, g % per
                gz, gx, gc = p % deep, (p // deep) % 2, p // (2 * deep)
                r = (gz * 2 + gx) * 2 + gc
                line = table_t[q, pl.ds(pl.multiple_of((r * per + e) * DS, DS), DS), :]
                both = jnp.concatenate([line[:, :half], line[:, half:]], axis=0)
                lines.append(jnp.concatenate([both, blank] if n == 0 else [blank, both], axis=1))
                ids.append(r * owned + q * per + e)
                places.append(pl.ds(pl.multiple_of(g * DS, DS), DS))
            hots, uppers = pair(*ids)
            made = jnp.dot(jnp.concatenate(lines, axis=0), hots, preferred_element_type=F32)
            for n in range(2):
                a = 2 * n * DS
                chosen = jnp.where(uppers[n], made[a + DS:a + 2 * DS], made[a:a + DS])
                recon[places[n], :] = chosen.astype(BF16)
            return carry

        lax.fori_loop(0, n_row * per // 8, one, 0)

    def gradient(q):
        g_part[q] = inverse * jnp.dot(recon[...], v_ref[...], preferred_element_type=F32)

    def start(copies):
        for copy in copies:
            copy.start()

    def wait(copies):
        for copy in copies:
            copy.wait()

    def stage(s, q):
        if s == 0:
            core_copy(q).start()
        elif s == 1:
            core_copy(q).wait()
            sum_core[q] = part[q, :, pl.ds(core * half, half)] + got_core[q]
            start(feat_copies(q))
        elif s == 2:
            wait(feat_copies(q))
            total = sum_core[q, 0]
            for i in range(n_feat - 1):
                total = total + got_feat[q, i]
            sum_feat[q, 0] = total
            sum_feat[q, 1] = sum_core[q, n_feat]
            x_copy(q).start()
        elif s == 3:
            x_copy(q).wait()
            sum_x[q] = sum_feat[q, :, pl.ds(x * quarter, quarter)] + got_x[q]
            start(z_copies(q))
        elif s == 4:
            wait(z_copies(q))
            total = sum_x[q, :, pl.ds(z * own, own)]
            for i in range(deep - 1):
                total = total + got_z[q, i]
            mean = total[0] / (total[1] + 1.0)
            cent_ref[q] = mean
            table[q, core, me_f, x, z] = mean.astype(BF16)
            start(table_z(q))
        elif s == 5:
            wait(table_z(q))
            start(table_x(q))
        elif s == 6:
            wait(table_x(q))
            start(table_feat(q))
        elif s == 7:
            wait(table_feat(q))
            start(table_core(q))
        else:
            wait(table_core(q))
            for f in range(n_feat):
                turned = table[q, :, f].astype(F32).reshape(K, LANES).T.astype(BF16)
                table_t[q, f * LANES:(f + 1) * LANES, :] = turned

    def g_stage(s, q):
        if s == 0:
            g_core_copy(q).start()
        elif s == 1:
            g_core_copy(q).wait()
            g_sum_core[q] = g_part[q, pl.ds(core * g_half, g_half)] + g_got_core[q]
            g_x_copy(q).start()
        elif s == 2:
            g_x_copy(q).wait()
            g_sum_x[q] = g_sum_core[q, pl.ds(x * g_quarter, g_quarter)] + g_got_x[q]
            start(g_z_copies(q))
        else:
            wait(g_z_copies(q))
            total = g_sum_x[q, pl.ds(z * deal, deal)]
            for i in range(deep - 1):
                total = total + g_got_z[q, i]
            grad_ref[pl.ds(pl.multiple_of(q * deal, deal), deal), :] = total

    each = 2 * n_feat
    steps = tiles * each
    stages = 9
    after = max([steps] + [each * (q + 1) + stages - 4 * q for q in range(tiles)])
    ends = after + 4 * tiles

    def step(t, carry):
        for s in reversed(range(4)):
            g = t - after - 4 - s

            @pl.when((g >= 0) & (g % 4 == 0) & (g // 4 < tiles))
            def _():
                g_stage(s, g // 4)

        for s in reversed(range(stages)):
            g = t - each - s

            @pl.when((g >= 0) & (g % each == 0) & (g // each < tiles))
            def _():
                stage(s, g // each)

        @pl.when(t < steps)
        def _():
            q = t // each

            @pl.when(t % each == 0)
            def _():
                build(q)

            sum_half((n_feat - 1) - (t % each) // 2, q, t % 2)

        @pl.when((t >= after) & (t < ends))
        def _():
            u = t - after
            rebuild(u // 4, (u % 4) * (n_row * per // 4))

            @pl.when(u % 4 == 3)
            def _():
                gradient(u // 4)

        return carry

    lax.fori_loop(0, ends + 4, step, 0)


def shards(vectors, rotation, codes, live_rows):
    rows, local = vectors.shape
    groups = codes.shape[1]
    n_row, n_feat = lax.axis_size("row"), lax.axis_size("feat")
    deep, own, tiles = n_row // 4, K // n_row, local // LANES
    out_rows = n_feat * local // n_row
    per = PER * n_feat // n_row
    deal = per * DS
    g_rows = n_row * deal
    others, far = max(n_feat - 1, 1), max(deep - 1, 1)
    keep = jnp.arange(rows, dtype=jnp.int32) < live_rows[0]
    owner, inside = codes // own, codes % own
    place = ((owner % 2 * 2 + owner // 2 % 2) * deep + owner // 4) * own + inside
    coded = jnp.where(keep[:, None], place, -1).astype(BF16).T
    vmem = pltpu.VMEM
    sem = pltpu.SemaphoreType.DMA
    means, grad_t = pl.pallas_call(
        functools.partial(kernel, n_row, n_feat, 1.0 / (rows * n_row)),
        out_shape=(
            jax.ShapeDtypeStruct((tiles, own, LANES), F32),
            jax.ShapeDtypeStruct((out_rows, local), F32),
        ),
        in_specs=[pl.BlockSpec(memory_space=vmem)] * 3,
        out_specs=(pl.BlockSpec(memory_space=vmem),) * 2,
        scratch_shapes=[
            vmem((others, groups, rows), BF16),
            vmem((n_feat * groups, rows), F32),
            vmem((K // 2, LANES), BF16),
            vmem((tiles, n_feat * LANES, local), BF16),
            vmem((n_feat * PER, 3 * DS, rows), BF16),
            vmem((LANES, K), F32),
            vmem((LANES, K), F32),
            vmem((tiles, n_feat + 1, K, LANES), F32),
            vmem((tiles, n_feat + 1, K // 2, LANES), F32),
            vmem((tiles, n_feat + 1, K // 2, LANES), F32),
            vmem((tiles, others, K // 2, LANES), F32),
            vmem((tiles, 2, K // 2, LANES), F32),
            vmem((tiles, 2, K // 4, LANES), F32),
            vmem((tiles, 2, K // 4, LANES), F32),
            vmem((tiles, far, 2, own, LANES), F32),
            vmem((tiles, 2, n_feat, 2, deep, own, LANES), BF16),
            vmem((tiles, n_feat * LANES, K), BF16),
            vmem((g_rows, rows), BF16),
            vmem((tiles, g_rows, local), F32),
            vmem((tiles, g_rows // 2, local), F32),
            vmem((tiles, g_rows // 2, local), F32),
            vmem((tiles, g_rows // 4, local), F32),
            vmem((tiles, g_rows // 4, local), F32),
            vmem((tiles, far, deal, local), F32),
            sem((others, 2)),
            sem((tiles, 2)),
            sem((tiles, others, 2)),
            sem((tiles, 2)),
            sem((tiles, far, 2)),
            sem((tiles, far, 2)),
            sem((tiles, 2)),
            sem((tiles, others, 2)),
            sem((tiles, 2)),
            sem((tiles, 2)),
            sem((tiles, 2)),
            sem((tiles, far, 2)),
        ],
        compiler_params=pltpu.CompilerParams(
            collective_id=0, has_side_effects=True, vmem_limit_bytes=63 * 1024 * 1024
        ),
    )(vectors, rotation, coded)
    split = means.reshape(tiles, own, PER // per, per, DS)
    return split.transpose(1, 2, 0, 3, 4).reshape(own, local), grad_t


def solution(mesh):
    return jax.shard_map(
        shards,
        mesh=mesh,
        in_specs=(P("row", "feat"), P("feat", None), P("row", "feat"), P("row")),
        out_specs=(P("row", "feat"), P("row", "feat")),
        check_vma=False,
    )
```

```python
import functools

import jax
import jax.numpy as jnp
from jax import lax
from jax.experimental import pallas as pl
from jax.experimental.pallas import tpu as pltpu
from jax.sharding import PartitionSpec as P

K = 256
DS = 16
LANES = 128
PER = LANES // DS
MESH = pl.DeviceIdType.MESH
F32 = jnp.float32
BF16 = jnp.bfloat16


def one_hot(code_row, kinds):
    return jnp.where(code_row.astype(BF16) == kinds, jnp.ones((), BF16), jnp.zeros((), BF16))


def kernel(
    n_row, n_feat, inverse,
    v_ref, r_ref, codes_ref, cent_ref, grad_ref,
    code_in, codes_all, kinds_ref, r_tiles, weights, sums_t, counts_t,
    part, got_core, sum_core, got,
    table, table_t, recon,
    g_part, g_got_core, g_sum_core, g_got_x, g_sum_x, g_got_z,
    code_sems, s_core, s_peer, t_peer, t_core, g_core, g_x, g_z,
):
    rows, local = v_ref.shape
    groups = codes_ref.shape[0]
    deep = n_row // 4
    own = K // n_row
    tiles = local // LANES
    per = PER * n_feat // n_row
    owned = tiles * per
    half, quarter = K // 2, K // 4
    me_r, me_f = lax.axis_index("row"), lax.axis_index("feat")
    core, x, z = me_r % 2, (me_r // 2) % 2, me_r // 4

    def at(zz, xx, cc):
        return {"row": (zz * 2 + xx) * 2 + cc}

    sib_core, sib_x = at(z, x, 1 - core), at(z, 1 - x, core)
    z_peers = [at((z + s) % deep, x, core) for s in range(1, deep)]
    f_peers = [{"feat": (me_f + s) % n_feat} for s in range(1, n_feat)]

    barrier = pltpu.get_barrier_semaphore()
    pl.semaphore_signal(barrier, inc=1, device_id=sib_core, device_id_type=MESH)

    def peer(df, n):
        place = at((z + n % deep) % deep, (x + n // deep) % 2, core)
        return {**place, "feat": (me_f + df) % n_feat}

    def each_peer(act):
        for df in range(n_feat):
            def one(n, carry, df=df):
                act(df, n)
                return carry

            lax.fori_loop(0 if df else 1, 2 * deep, one, 0)

    each_peer(lambda df, n: pl.semaphore_signal(
        barrier, inc=1, device_id=peer(df, n), device_id_type=MESH))
    pl.semaphore_wait(barrier, 2 * deep * n_feat)

    def remote(src, dst, sems, peer):
        return pltpu.make_async_remote_copy(
            src_ref=src, dst_ref=dst, send_sem=sems.at[0], recv_sem=sems.at[1],
            device_id=peer, device_id_type=MESH,
        )

    sends = [
        remote(codes_ref, code_in.at[s], code_sems.at[s], f_peers[s])
        for s in range(n_feat - 1)
    ]
    for copy in sends:
        copy.start()
    kinds_ref[...] = lax.broadcasted_iota(jnp.int32, (half, LANES), 0).astype(F32).astype(BF16)
    weights[:, 2 * DS:, :] = jnp.ones((n_feat * PER, DS, rows), BF16)
    codes_all[pl.ds(pl.multiple_of(me_f * groups, 8), groups), :] = codes_ref[...].astype(F32)

    def member(i, q):
        return (i // per) * owned + q * per + i % per

    for f in range(n_feat):
        block = r_ref[:, f * local:(f + 1) * local].astype(F32)
        for q in range(tiles):
            r_tiles[q, f * LANES:(f + 1) * LANES] = jnp.concatenate(
                [block[:, member(i, q) * DS:(member(i, q) + 1) * DS] for i in range(PER)], axis=1
            ).T.astype(BF16)
    for s in range(n_feat - 1):
        sends[s].wait()
        source = (me_f - (s + 1) + n_feat) % n_feat
        codes_all[pl.ds(pl.multiple_of(source * groups, 8), groups), :] = code_in[s].astype(F32)

    nt = (((1,), (1,)), ((), ()))

    def pair(first, second):
        kinds = jnp.concatenate([kinds_ref[...]] * (rows // LANES), axis=1)
        hots, uppers = [], []
        for m in (first, second):
            row = codes_all[pl.ds(m, 1), :]
            upper = row >= half
            hots.append(one_hot(jnp.where(upper, row - half, row), kinds))
            uppers.append(upper)
        return jnp.concatenate(hots, axis=0), uppers

    def build(q):
        rot = lax.dot_general(r_tiles[q], v_ref[...], nt, preferred_element_type=F32)
        high = rot.astype(BF16)
        low = (rot - high.astype(F32)).astype(BF16)
        for i in range(n_feat * PER):
            weights[i, :DS] = high[i * DS:(i + 1) * DS]
            weights[i, DS:2 * DS] = low[i * DS:(i + 1) * DS]

    def sum_pair(f, q, i):
        ids = [f * groups + member(i + n, q) for n in range(2)]
        hots, uppers = pair(*ids)
        lines = []
        for n in range(2):
            line = weights[f * PER + i + n]
            up = jnp.where(uppers[n], 1.0, 0.0)
            lines += [line * (1.0 - up).astype(BF16), line * up.astype(BF16)]
        made = lax.dot_general(
            jnp.concatenate(lines, axis=0), hots, nt, preferred_element_type=F32
        )
        for n in range(2):
            features = pl.ds(pl.multiple_of((i + n) * DS, DS), DS)
            for side in range(2):
                at_row = (2 * n + side) * 3 * DS
                both = made[at_row:at_row + 3 * DS, n * half:(n + 1) * half]
                positions = slice(side * half, (side + 1) * half)
                sums_t[features, positions] = both[:DS] + both[DS:2 * DS]
                counts_t[features, positions] = both[2 * DS:]

    def sum_half(df, q, h):
        f = (me_f + df) % n_feat

        def one(i, carry):
            sum_pair(f, q, h * (PER // 2) + 2 * i)
            return carry

        lax.fori_loop(0, PER // 4, one, 0)

        @pl.when(h == 1)
        def _():
            part[q, df + 1] = sums_t[...].T

            @pl.when(df == 0)
            def _():
                part[q, 0] = counts_t[...].T

    def core_copy(q):
        return remote(
            part.at[q, :, pl.ds((1 - core) * half, half)], got_core.at[q], s_core.at[q], sib_core
        )

    def peer_copy(q, df, n):
        px, pz = (x + n // deep) % 2, (z + n % deep) % deep
        piece = pl.ds((px * deep + pz) * own, own)
        slabs = pl.ds(df + 1, 1) if df else pl.ds(0, 2)
        lands = pl.ds(1, 1) if df else pl.ds(0, 2)
        return remote(
            sum_core.at[q, slabs, piece], got.at[q, df, n, lands], s_peer.at[q, df, n], peer(df, n)
        )

    def table_copy(q, df, n):
        piece = table.at[q, core, me_f, x, z]
        return remote(piece, piece, t_peer.at[q, df, n], peer(df, n))

    def table_core(q):
        piece = table.at[q, core]
        return remote(piece, piece, t_core.at[q], sib_core)

    deal = per * DS
    g_half, g_quarter = n_row * deal // 2, n_row * deal // 4

    def g_core_copy(q):
        return remote(
            g_part.at[q, pl.ds((1 - core) * g_half, g_half)], g_got_core.at[q], g_core.at[q], sib_core
        )

    def g_x_copy(q):
        return remote(
            g_sum_core.at[q, pl.ds((1 - x) * g_quarter, g_quarter)], g_got_x.at[q], g_x.at[q], sib_x
        )

    def g_z_copies(q):
        return [
            remote(
                g_sum_x.at[q, pl.ds(((z + s) % deep) * deal, deal)], g_got_z.at[q, s - 1],
                g_z.at[q, s - 1], z_peers[s - 1],
            )
            for s in range(1, deep)
        ]

    def rebuild(q, lo):
        def one(i, carry):
            places, ids, lines = [], [], []
            blank = jnp.zeros((2 * DS, half), BF16)
            for n in range(2):
                g = lo + 2 * i + n
                p, e = g // per, g % per
                gz, gx, gc = p % deep, (p // deep) % 2, p // (2 * deep)
                r = (gz * 2 + gx) * 2 + gc
                line = table_t[q, pl.ds(pl.multiple_of((r * per + e) * DS, DS), DS), :]
                both = jnp.concatenate([line[:, :half], line[:, half:]], axis=0)
                lines.append(jnp.concatenate([both, blank] if n == 0 else [blank, both], axis=1))
                ids.append(r * owned + q * per + e)
                places.append(pl.ds(pl.multiple_of(g * DS, DS), DS))
            hots, uppers = pair(*ids)
            made = jnp.dot(jnp.concatenate(lines, axis=0), hots, preferred_element_type=F32)
            for n in range(2):
                a = 2 * n * DS
                chosen = jnp.where(uppers[n], made[a + DS:a + 2 * DS], made[a:a + DS])
                recon[places[n], :] = chosen.astype(BF16)
            return carry

        lax.fori_loop(0, n_row * per // 8, one, 0)

    def gradient(q):
        g_part[q] = inverse * jnp.dot(recon[...], v_ref[...], preferred_element_type=F32)

    def start(copies):
        for copy in copies:
            copy.start()

    def wait(copies):
        for copy in copies:
            copy.wait()

    def stage(s, q):
        if s == 0:
            core_copy(q).start()
        elif s == 1:
            core_copy(q).wait()
            sum_core[q] = part[q, :, pl.ds(core * half, half)] + got_core[q]
            each_peer(lambda df, n: peer_copy(q, df, n).start())
        elif s == 2:
            each_peer(lambda df, n: peer_copy(q, df, n).wait())
            mine = pl.ds((x * deep + z) * own, own)
            count, total = sum_core[q, 0, mine], sum_core[q, 1, mine]
            for df in range(n_feat):
                for n in range(0 if df else 1, 2 * deep):
                    total = total + got[q, df, n, 1]
                    if df == 0:
                        count = count + got[q, df, n, 0]
            mean = total / (count + 1.0)
            cent_ref[q] = mean
            table[q, core, me_f, x, z] = mean.astype(BF16)
            each_peer(lambda df, n: table_copy(q, df, n).start())
        elif s == 3:
            each_peer(lambda df, n: table_copy(q, df, n).wait())
            table_core(q).start()
        else:
            table_core(q).wait()
            for f in range(n_feat):
                turned = table[q, :, f].astype(F32).reshape(K, LANES).T.astype(BF16)
                table_t[q, f * LANES:(f + 1) * LANES, :] = turned

    def g_stage(s, q):
        if s == 0:
            g_core_copy(q).start()
        elif s == 1:
            g_core_copy(q).wait()
            g_sum_core[q] = g_part[q, pl.ds(core * g_half, g_half)] + g_got_core[q]
            g_x_copy(q).start()
        elif s == 2:
            g_x_copy(q).wait()
            g_sum_x[q] = g_sum_core[q, pl.ds(x * g_quarter, g_quarter)] + g_got_x[q]
            start(g_z_copies(q))
        else:
            wait(g_z_copies(q))
            total = g_sum_x[q, pl.ds(z * deal, deal)]
            for i in range(deep - 1):
                total = total + g_got_z[q, i]
            grad_ref[pl.ds(pl.multiple_of(q * deal, deal), deal), :] = total

    each = 2 * n_feat
    steps = tiles * each
    stages, gap = 5, 3
    after = max([steps] + [each * (q + 1) + gap * (stages - 1) - 4 * q for q in range(tiles)])
    ends = after + 4 * tiles

    def step(t, carry):
        for s in reversed(range(4)):
            g = t - after - 4 - gap * s

            @pl.when((g >= 0) & (g % 4 == 0) & (g // 4 < tiles))
            def _():
                g_stage(s, g // 4)

        for s in reversed(range(stages)):
            g = t - each - gap * s

            @pl.when((g >= 0) & (g % each == 0) & (g // each < tiles))
            def _():
                stage(s, g // each)

        @pl.when(t < steps)
        def _():
            q = t // each

            @pl.when(t % each == 0)
            def _():
                build(q)

            sum_half((n_feat - 1) - (t % each) // 2, q, t % 2)

        @pl.when((t >= after) & (t < ends))
        def _():
            u = t - after
            rebuild(u // 4, (u % 4) * (n_row * per // 4))

            @pl.when(u % 4 == 3)
            def _():
                gradient(u // 4)

        return carry

    lax.fori_loop(0, ends + 1 + 3 * gap, step, 0)


def shards(vectors, rotation, codes, live_rows):
    rows, local = vectors.shape
    groups = codes.shape[1]
    n_row, n_feat = lax.axis_size("row"), lax.axis_size("feat")
    deep, own, tiles = n_row // 4, K // n_row, local // LANES
    out_rows = n_feat * local // n_row
    per = PER * n_feat // n_row
    deal = per * DS
    g_rows = n_row * deal
    others, far = max(n_feat - 1, 1), max(deep - 1, 1)
    keep = jnp.arange(rows, dtype=jnp.int32) < live_rows[0]
    owner, inside = codes // own, codes % own
    place = ((owner % 2 * 2 + owner // 2 % 2) * deep + owner // 4) * own + inside
    coded = jnp.where(keep[:, None], place, -1).astype(BF16).T
    vmem = pltpu.VMEM
    sem = pltpu.SemaphoreType.DMA
    means, grad_t = pl.pallas_call(
        functools.partial(kernel, n_row, n_feat, 1.0 / (rows * n_row)),
        out_shape=(
            jax.ShapeDtypeStruct((tiles, own, LANES), F32),
            jax.ShapeDtypeStruct((out_rows, local), F32),
        ),
        in_specs=[pl.BlockSpec(memory_space=vmem)] * 3,
        out_specs=(pl.BlockSpec(memory_space=vmem),) * 2,
        scratch_shapes=[
            vmem((others, groups, rows), BF16),
            vmem((n_feat * groups, rows), F32),
            vmem((K // 2, LANES), BF16),
            vmem((tiles, n_feat * LANES, local), BF16),
            vmem((n_feat * PER, 3 * DS, rows), BF16),
            vmem((LANES, K), F32),
            vmem((LANES, K), F32),
            vmem((tiles, n_feat + 1, K, LANES), F32),
            vmem((tiles, n_feat + 1, K // 2, LANES), F32),
            vmem((tiles, n_feat + 1, K // 2, LANES), F32),
            vmem((tiles, n_feat, 2 * deep, 2, own, LANES), F32),
            vmem((tiles, 2, n_feat, 2, deep, own, LANES), BF16),
            vmem((tiles, n_feat * LANES, K), BF16),
            vmem((g_rows, rows), BF16),
            vmem((tiles, g_rows, local), F32),
            vmem((tiles, g_rows // 2, local), F32),
            vmem((tiles, g_rows // 2, local), F32),
            vmem((tiles, g_rows // 4, local), F32),
            vmem((tiles, g_rows // 4, local), F32),
            vmem((tiles, far, deal, local), F32),
            sem((others, 2)),
            sem((tiles, 2)),
            sem((tiles, n_feat, 2 * deep, 2)),
            sem((tiles, n_feat, 2 * deep, 2)),
            sem((tiles, 2)),
            sem((tiles, 2)),
            sem((tiles, 2)),
            sem((tiles, far, 2)),
        ],
        compiler_params=pltpu.CompilerParams(
            collective_id=0, has_side_effects=True, vmem_limit_bytes=63 * 1024 * 1024
        ),
    )(vectors, rotation, coded)
    split = means.reshape(tiles, own, PER // per, per, DS)
    return split.transpose(1, 2, 0, 3, 4).reshape(own, local), grad_t


def solution(mesh):
    return jax.shard_map(
        shards,
        mesh=mesh,
        in_specs=(P("row", "feat"), P("feat", None), P("row", "feat"), P("row")),
        out_specs=(P("row", "feat"), P("row", "feat")),
        check_vma=False,
    )
```

```python
import functools

import jax
import jax.numpy as jnp
from jax import lax
from jax.experimental import pallas as pl
from jax.experimental.pallas import tpu as pltpu
from jax.sharding import PartitionSpec as P

K = 256
DS = 16
LANES = 128
PER = LANES // DS
MESH = pl.DeviceIdType.MESH
F32 = jnp.float32
BF16 = jnp.bfloat16


def one_hot(code_row, kinds):
    return jnp.where(code_row.astype(BF16) == kinds, jnp.ones((), BF16), jnp.zeros((), BF16))


def kernel(
    n_row, n_feat, inverse,
    v_ref, r_ref, codes_ref, cent_ref, grad_ref,
    code_in, codes_all, kinds_ref, r_tiles, weights, sums_t, counts_t,
    part, got_core, sum_core, got,
    table, table_t, recon,
    g_part, g_got_core, g_sum_core, g_got_x, g_sum_x, g_got_z,
    code_sems, s_core, s_peer, t_peer, t_core, g_core, g_x, g_z,
):
    rows, local = v_ref.shape
    groups = codes_ref.shape[0]
    deep = n_row // 4
    own = K // n_row
    tiles = local // LANES
    per = PER * n_feat // n_row
    owned = tiles * per
    half, quarter = K // 2, K // 4
    me_r, me_f = lax.axis_index("row"), lax.axis_index("feat")
    core, x, z = me_r % 2, (me_r // 2) % 2, me_r // 4

    def at(zz, xx, cc):
        return {"row": (zz * 2 + xx) * 2 + cc}

    sib_core, sib_x = at(z, x, 1 - core), at(z, 1 - x, core)
    z_peers = [at((z + s) % deep, x, core) for s in range(1, deep)]
    f_peers = [{"feat": (me_f + s) % n_feat} for s in range(1, n_feat)]

    barrier = pltpu.get_barrier_semaphore()
    pl.semaphore_signal(barrier, inc=1, device_id=sib_core, device_id_type=MESH)

    def peer(df, n):
        place = at((z + n % deep) % deep, (x + n // deep) % 2, core)
        return {**place, "feat": (me_f + df) % n_feat}

    def each_peer(act):
        for df in range(n_feat):
            def one(n, carry, df=df):
                act(df, n)
                return carry

            lax.fori_loop(0 if df else 1, 2 * deep, one, 0)

    each_peer(lambda df, n: pl.semaphore_signal(
        barrier, inc=1, device_id=peer(df, n), device_id_type=MESH))
    pl.semaphore_wait(barrier, 2 * deep * n_feat)

    def remote(src, dst, sems, peer):
        return pltpu.make_async_remote_copy(
            src_ref=src, dst_ref=dst, send_sem=sems.at[0], recv_sem=sems.at[1],
            device_id=peer, device_id_type=MESH,
        )

    sends = [
        remote(codes_ref, code_in.at[s], code_sems.at[s], f_peers[s])
        for s in range(n_feat - 1)
    ]
    for copy in sends:
        copy.start()
    kinds_ref[...] = lax.broadcasted_iota(jnp.int32, (half, LANES), 0).astype(F32).astype(BF16)
    weights[:, 2 * DS:, :] = jnp.ones((n_feat * PER, DS, rows), BF16)
    codes_all[pl.ds(pl.multiple_of(me_f * groups, 8), groups), :] = codes_ref[...].astype(F32)

    def member(i, q):
        return (i // per) * owned + q * per + i % per

    for f in range(n_feat):
        block = r_ref[:, f * local:(f + 1) * local].astype(F32)
        for q in range(tiles):
            r_tiles[q, f * LANES:(f + 1) * LANES] = jnp.concatenate(
                [block[:, member(i, q) * DS:(member(i, q) + 1) * DS] for i in range(PER)], axis=1
            ).T.astype(BF16)
    for s in range(n_feat - 1):
        sends[s].wait()
        source = (me_f - (s + 1) + n_feat) % n_feat
        codes_all[pl.ds(pl.multiple_of(source * groups, 8), groups), :] = code_in[s].astype(F32)

    nt = (((1,), (1,)), ((), ()))

    def pair(first, second):
        kinds = jnp.concatenate([kinds_ref[...]] * (rows // LANES), axis=1)
        hots, uppers = [], []
        for m in (first, second):
            row = codes_all[pl.ds(m, 1), :]
            upper = row >= half
            hots.append(one_hot(jnp.where(upper, row - half, row), kinds))
            uppers.append(upper)
        return jnp.concatenate(hots, axis=0), uppers

    def build(q):
        rot = lax.dot_general(r_tiles[q], v_ref[...], nt, preferred_element_type=F32)
        high = rot.astype(BF16)
        low = (rot - high.astype(F32)).astype(BF16)
        for i in range(n_feat * PER):
            weights[i, :DS] = high[i * DS:(i + 1) * DS]
            weights[i, DS:2 * DS] = low[i * DS:(i + 1) * DS]

    def sum_pair(f, q, i):
        ids = [f * groups + member(i + n, q) for n in range(2)]
        hots, uppers = pair(*ids)
        lines = []
        for n in range(2):
            line = weights[f * PER + i + n]
            up = jnp.where(uppers[n], 1.0, 0.0)
            lines += [line * (1.0 - up).astype(BF16), line * up.astype(BF16)]
        made = lax.dot_general(
            jnp.concatenate(lines, axis=0), hots, nt, preferred_element_type=F32
        )
        for n in range(2):
            features = pl.ds(pl.multiple_of((i + n) * DS, DS), DS)
            for side in range(2):
                at_row = (2 * n + side) * 3 * DS
                both = made[at_row:at_row + 3 * DS, n * half:(n + 1) * half]
                positions = slice(side * half, (side + 1) * half)
                sums_t[features, positions] = both[:DS] + both[DS:2 * DS]
                counts_t[features, positions] = both[2 * DS:]

    def sum_half(df, q, h):
        f = (me_f + df) % n_feat

        def one(i, carry):
            sum_pair(f, q, h * (PER // 2) + 2 * i)
            return carry

        lax.fori_loop(0, PER // 4, one, 0, unroll=True)

        @pl.when(h == 1)
        def _():
            part[q, df + 1] = sums_t[...].T

            @pl.when(df == 0)
            def _():
                part[q, 0] = counts_t[...].T

    def core_copy(q):
        return remote(
            part.at[q, :, pl.ds((1 - core) * half, half)], got_core.at[q], s_core.at[q], sib_core
        )

    def peer_copy(q, df, n):
        px, pz = (x + n // deep) % 2, (z + n % deep) % deep
        piece = pl.ds((px * deep + pz) * own, own)
        slabs = pl.ds(df + 1, 1) if df else pl.ds(0, 2)
        lands = pl.ds(1, 1) if df else pl.ds(0, 2)
        return remote(
            sum_core.at[q, slabs, piece], got.at[q, df, n, lands], s_peer.at[q, df, n], peer(df, n)
        )

    def table_copy(q, df, n):
        piece = table.at[q, core, me_f, x, z]
        return remote(piece, piece, t_peer.at[q, df, n], peer(df, n))

    def table_core(q):
        piece = table.at[q, core]
        return remote(piece, piece, t_core.at[q], sib_core)

    deal = per * DS
    g_half, g_quarter = n_row * deal // 2, n_row * deal // 4

    def g_core_copy(q):
        return remote(
            g_part.at[q, pl.ds((1 - core) * g_half, g_half)], g_got_core.at[q], g_core.at[q], sib_core
        )

    def g_x_copy(q):
        return remote(
            g_sum_core.at[q, pl.ds((1 - x) * g_quarter, g_quarter)], g_got_x.at[q], g_x.at[q], sib_x
        )

    def g_z_copies(q):
        return [
            remote(
                g_sum_x.at[q, pl.ds(((z + s) % deep) * deal, deal)], g_got_z.at[q, s - 1],
                g_z.at[q, s - 1], z_peers[s - 1],
            )
            for s in range(1, deep)
        ]

    def rebuild(q, lo):
        def one(i, carry):
            places, ids, lines = [], [], []
            blank = jnp.zeros((2 * DS, half), BF16)
            for n in range(2):
                g = lo + 2 * i + n
                p, e = g // per, g % per
                gz, gx, gc = p % deep, (p // deep) % 2, p // (2 * deep)
                r = (gz * 2 + gx) * 2 + gc
                line = table_t[q, pl.ds(pl.multiple_of((r * per + e) * DS, DS), DS), :]
                both = jnp.concatenate([line[:, :half], line[:, half:]], axis=0)
                lines.append(jnp.concatenate([both, blank] if n == 0 else [blank, both], axis=1))
                ids.append(r * owned + q * per + e)
                places.append(pl.ds(pl.multiple_of(g * DS, DS), DS))
            hots, uppers = pair(*ids)
            made = jnp.dot(jnp.concatenate(lines, axis=0), hots, preferred_element_type=F32)
            for n in range(2):
                a = 2 * n * DS
                chosen = jnp.where(uppers[n], made[a + DS:a + 2 * DS], made[a:a + DS])
                recon[places[n], :] = chosen.astype(BF16)
            return carry

        lax.fori_loop(0, n_row * per // 8, one, 0, unroll=2)

    def gradient(q):
        g_part[q] = inverse * jnp.dot(recon[...], v_ref[...], preferred_element_type=F32)

    def start(copies):
        for copy in copies:
            copy.start()

    def wait(copies):
        for copy in copies:
            copy.wait()

    def stage(s, q):
        if s == 0:
            core_copy(q).start()
        elif s == 1:
            core_copy(q).wait()
            sum_core[q] = part[q, :, pl.ds(core * half, half)] + got_core[q]
            each_peer(lambda df, n: peer_copy(q, df, n).start())
        elif s == 2:
            each_peer(lambda df, n: peer_copy(q, df, n).wait())
            mine = pl.ds((x * deep + z) * own, own)
            count, total = sum_core[q, 0, mine], sum_core[q, 1, mine]
            for df in range(n_feat):
                for n in range(0 if df else 1, 2 * deep):
                    total = total + got[q, df, n, 1]
                    if df == 0:
                        count = count + got[q, df, n, 0]
            mean = total / (count + 1.0)
            cent_ref[q] = mean
            table[q, core, me_f, x, z] = mean.astype(BF16)
            each_peer(lambda df, n: table_copy(q, df, n).start())
        elif s == 3:
            each_peer(lambda df, n: table_copy(q, df, n).wait())
            table_core(q).start()
        else:
            table_core(q).wait()
            for f in range(n_feat):
                turned = table[q, :, f].astype(F32).reshape(K, LANES).T.astype(BF16)
                table_t[q, f * LANES:(f + 1) * LANES, :] = turned

    def g_stage(s, q):
        if s == 0:
            g_core_copy(q).start()
        elif s == 1:
            g_core_copy(q).wait()
            g_sum_core[q] = g_part[q, pl.ds(core * g_half, g_half)] + g_got_core[q]
            g_x_copy(q).start()
        elif s == 2:
            g_x_copy(q).wait()
            g_sum_x[q] = g_sum_core[q, pl.ds(x * g_quarter, g_quarter)] + g_got_x[q]
            start(g_z_copies(q))
        else:
            wait(g_z_copies(q))
            total = g_sum_x[q, pl.ds(z * deal, deal)]
            for i in range(deep - 1):
                total = total + g_got_z[q, i]
            grad_ref[pl.ds(pl.multiple_of(q * deal, deal), deal), :] = total

    each = 2 * n_feat
    steps = tiles * each
    stages, gap = 5, 3
    after = max([steps] + [each * (q + 1) + gap * (stages - 1) - 4 * q for q in range(tiles)])
    ends = after + 4 * tiles

    def step(t, carry):
        for s in reversed(range(4)):
            g = t - after - 4 - gap * s

            @pl.when((g >= 0) & (g % 4 == 0) & (g // 4 < tiles))
            def _():
                g_stage(s, g // 4)

        for s in reversed(range(stages)):
            g = t - each - gap * s

            @pl.when((g >= 0) & (g % each == 0) & (g // each < tiles))
            def _():
                stage(s, g // each)

        @pl.when(t < steps)
        def _():
            q = t // each

            @pl.when(t % each == 0)
            def _():
                build(q)

            sum_half((n_feat - 1) - (t % each) // 2, q, t % 2)

        @pl.when((t >= after) & (t < ends))
        def _():
            u = t - after
            rebuild(u // 4, (u % 4) * (n_row * per // 4))

            @pl.when(u % 4 == 3)
            def _():
                gradient(u // 4)

        return carry

    lax.fori_loop(0, ends + 1 + 3 * gap, step, 0)


def shards(vectors, rotation, codes, live_rows):
    rows, local = vectors.shape
    groups = codes.shape[1]
    n_row, n_feat = lax.axis_size("row"), lax.axis_size("feat")
    deep, own, tiles = n_row // 4, K // n_row, local // LANES
    out_rows = n_feat * local // n_row
    per = PER * n_feat // n_row
    deal = per * DS
    g_rows = n_row * deal
    others, far = max(n_feat - 1, 1), max(deep - 1, 1)
    keep = jnp.arange(rows, dtype=jnp.int32) < live_rows[0]
    owner, inside = codes // own, codes % own
    place = ((owner % 2 * 2 + owner // 2 % 2) * deep + owner // 4) * own + inside
    coded = jnp.where(keep[:, None], place, -1).astype(BF16).T
    vmem = pltpu.VMEM
    sem = pltpu.SemaphoreType.DMA
    means, grad_t = pl.pallas_call(
        functools.partial(kernel, n_row, n_feat, 1.0 / (rows * n_row)),
        out_shape=(
            jax.ShapeDtypeStruct((tiles, own, LANES), F32),
            jax.ShapeDtypeStruct((out_rows, local), F32),
        ),
        in_specs=[pl.BlockSpec(memory_space=vmem)] * 3,
        out_specs=(pl.BlockSpec(memory_space=vmem),) * 2,
        scratch_shapes=[
            vmem((others, groups, rows), BF16),
            vmem((n_feat * groups, rows), F32),
            vmem((K // 2, LANES), BF16),
            vmem((tiles, n_feat * LANES, local), BF16),
            vmem((n_feat * PER, 3 * DS, rows), BF16),
            vmem((LANES, K), F32),
            vmem((LANES, K), F32),
            vmem((tiles, n_feat + 1, K, LANES), F32),
            vmem((tiles, n_feat + 1, K // 2, LANES), F32),
            vmem((tiles, n_feat + 1, K // 2, LANES), F32),
            vmem((tiles, n_feat, 2 * deep, 2, own, LANES), F32),
            vmem((tiles, 2, n_feat, 2, deep, own, LANES), BF16),
            vmem((tiles, n_feat * LANES, K), BF16),
            vmem((g_rows, rows), BF16),
            vmem((tiles, g_rows, local), F32),
            vmem((tiles, g_rows // 2, local), F32),
            vmem((tiles, g_rows // 2, local), F32),
            vmem((tiles, g_rows // 4, local), F32),
            vmem((tiles, g_rows // 4, local), F32),
            vmem((tiles, far, deal, local), F32),
            sem((others, 2)),
            sem((tiles, 2)),
            sem((tiles, n_feat, 2 * deep, 2)),
            sem((tiles, n_feat, 2 * deep, 2)),
            sem((tiles, 2)),
            sem((tiles, 2)),
            sem((tiles, 2)),
            sem((tiles, far, 2)),
        ],
        compiler_params=pltpu.CompilerParams(
            collective_id=0, has_side_effects=True, vmem_limit_bytes=63 * 1024 * 1024
        ),
    )(vectors, rotation, coded)
    split = means.reshape(tiles, own, PER // per, per, DS)
    return split.transpose(1, 2, 0, 3, 4).reshape(own, local), grad_t


def solution(mesh):
    return jax.shard_map(
        shards,
        mesh=mesh,
        in_specs=(P("row", "feat"), P("feat", None), P("row", "feat"), P("row")),
        out_specs=(P("row", "feat"), P("row", "feat")),
        check_vma=False,
    )
```
